32 devices in a mesh: seq: 8 (over z, x), head: 4 (over y, core).
Axes of the slice: x: 2, y: 2, z: 4, core: 2. Of those that a mesh axis runs over, the one named last changes fastest.
Arguments:
- hidden_in: bfloat16 [1024, 2048], P('seq', 'head'), may hold values from -6 to 6
- out_grad: float32 [1024, 2048], P('seq', 'head'), may hold values from -6 to 6
- expert_ids: int32 [1024, 8], P('seq'), may hold values from 0 to 63, all different within a row; in each aligned block of 128 rows (0 to 127, 128 to 255, ...) at most 32 rows name the same one
- route_weights: float32 [1024, 8], P('seq'), may hold values from 0.03 to 0.3
- w_gate: bfloat16 [64, 2048, 1024], P('seq', None, 'head'), may hold values from -0.125 to 0.125
- w_up: bfloat16 [64, 2048, 1024], P('seq', None, 'head'), may hold values from -0.125 to 0.125
- w_down: bfloat16 [64, 1024, 2048], P('seq', 'head'), may hold values from -0.1875 to 0.1875
- query_in: float32 [1024, 2048], P('seq', 'head'), may hold values from -6 to 6
- key_in: float32 [1024, 2048], P('seq', 'head'), may hold values from -6 to 6
- value_in: float32 [1024, 2048], P('seq', 'head'), may hold values from -6 to 6
- state_before: float32 [16, 128, 128], P('head'), may hold values from -192 to 192
- grad_after: float32 [16, 128, 128], P('head'), may hold values from -192 to 192
Outputs:
- grad_gate: bfloat16 [64, 2048, 1024], P('seq', None, 'head')
- grad_up: bfloat16 [64, 2048, 1024], P('seq', None, 'head')
- grad_down: bfloat16 [64, 1024, 2048], P('seq', 'head')
- grad_query: float32 [1024, 2048], P('seq', 'head')
- grad_key: float32 [1024, 2048], P('seq', 'head')
- grad_value: float32 [1024, 2048], P('seq', 'head')
The draws below stay inside these ranges and needn't reach their ends.
Inputs may be any that keep to these rules, and one draw needn't show every extreme that they name: `expert_ids`: each row names 8 different experts. Among the 128 rows of one index of seq (aligned blocks of 128 rows) no expert is named more than 32 times, a bound that some block reaches.
All inputs are finite; a program needn't handle non-finite values.
Results may differ from the reference program's by a relative error of at most 0.014.
Values may be sent and summed in bfloat16 or wider, within the bound.
A program may use at most 128 MiB of HBM per device.

```python
import math
import jax
import jax.numpy as jnp
import numpy as np
from jax import lax

D = 2048
FF = 1024
EXPERTS = 64
TOPK = 8
HEADS = 16
HD = 128
TOK_DEV = 128
TOKENS = 1024
CAP = 32
N_SEQ = 8
N_HEAD = 4


def steps_of(own_key, extent, shards, least, high):
    factor_of = 1.0
    for position, blocks in shards:
        draws = jax.random.uniform(jax.random.fold_in(jax.random.fold_in(own_key, 6), position), (blocks,), jnp.float32, least / len(shards), high / len(shards))
        factor_of = factor_of * jnp.repeat(jnp.exp(draws), extent[position] // blocks).reshape((-1,) + (1,) * (len(extent) - 1 - position))
    return factor_of


def routed_block(own_key, own, number, rows, number_of, top, limit, lean):
    order = jax.random.permutation(own_key, number_of)
    crowded, common = load_shares(number_of, rows * top, limit, lean, True), load_shares(number_of, rows * top, limit, lean, False)
    places = jnp.arange(number_of)

    def named(sizes, offset_by):
        used = int((sizes > 0).sum())
        fixed = max(1, used // 4)
        passed = fixed + (places - fixed + offset_by * (used - fixed)) % max(1, number_of - fixed)
        return jnp.zeros((number_of,), jnp.int32).at[order[jnp.where(places < fixed, places, passed)]].set(jnp.asarray(sizes, jnp.int32))

    sizes = jnp.where(number % 4 == 0, named(crowded, number // 4), named(common, number - number // 4 - 1))
    mixed = jax.random.permutation(jax.random.fold_in(own, 3), number_of)
    source_of, receiver = mixed[0:number_of // 2 * 2:2], mixed[1:number_of // 2 * 2:2]
    slack = jnp.minimum(sizes[source_of] - 1, limit - sizes[receiver]) // 2
    slack = jnp.where((source_of == order[0]) | (receiver == order[0]) | (sizes[receiver] == 0), 0, jnp.maximum(slack, 0))
    passed = jax.random.randint(jax.random.fold_in(own, 4), (number_of // 2,), 0, 1 << 20) % (slack + 1)
    sizes = sizes.at[source_of].add(-passed).at[receiver].add(passed)
    labels = jnp.searchsorted(jnp.cumsum(sizes), jnp.arange(rows * top), side="right").astype(jnp.int32)
    table = labels.reshape(top, rows).T
    table = table[jax.random.permutation(jax.random.fold_in(own, 1), rows)]
    offset_by = jax.random.randint(jax.random.fold_in(own, 2), (rows, 1), 0, top)
    return jnp.take_along_axis(table, (jnp.arange(top)[None, :] + offset_by) % top, axis=1)


def load_shares(amount, total, limit, skew, full):
    loads = [(1 << 20) // math.isqrt(rank ** skew) + 1 for rank in range(1, amount + 1)]
    largest = limit if full else min(limit, max(-(-total // amount), total * loads[0] // sum(loads)))
    least = 1 if total - largest >= amount - 1 else 0
    holding, spare = [largest] + [least] * (amount - 1), total - largest - least * (amount - 1)
    while spare > 0:
        candidates = [i for i in range(1, amount) if holding[i] < largest] or [i for i in range(1, amount) if holding[i] < limit]
        whole, remaining = sum([loads[i] for i in candidates]), spare
        for i in candidates:
            addition = min(limit - holding[i], max(1, remaining * loads[i] // whole), spare)
            holding[i] = holding[i] + addition
            spare = spare - addition
    return np.array(holding)


def noise(own_key, extent, spread, bound, shards=(), kind=jnp.bfloat16):
    values = spread * jax.random.normal(own_key, extent, jnp.float32)
    if shards:
        values = values * steps_of(own_key, extent, shards, -0.22, 0.18)
    return jnp.clip(values, -bound, bound).astype(kind)


def setup_inputs(seed: int = 0) -> dict:
    key_list = jax.random.split(jax.random.key(seed), 13)
    hidden_in = noise(key_list[0], (TOKENS, D), 1.0, 6.0, ((0, 8), (1, 4)))
    out_grad = noise(key_list[1], (TOKENS, D), 1.0, 6.0, ((0, 8), (1, 4)), jnp.float32)
    expert_ids_keys = jax.random.split(jax.random.fold_in(key_list[2], 1), TOKENS // TOK_DEV)
    expert_ids_turns = jax.random.permutation(jax.random.fold_in(key_list[2], 3), TOKENS // TOK_DEV)
    expert_ids = jax.vmap(lambda own, number: routed_block(jax.random.fold_in(key_list[2], 2), own, number, TOK_DEV, EXPERTS, TOPK, CAP, 2))(expert_ids_keys, expert_ids_turns).reshape((TOKENS, TOPK))
    route_weights = jnp.clip(jnp.exp(math.log(0.3) - 2.3025852 * jax.random.uniform(key_list[3], (TOKENS, TOPK), jnp.float32) ** steps_of(key_list[3], (TOKENS, TOPK), ((0, 8),), -0.2, 0.2)), 0.03, 0.3)
    w_gate = noise(key_list[4], (EXPERTS, D, FF), D ** -0.5, 0.125, ((0, 8), (2, 4)))
    w_up = noise(key_list[5], (EXPERTS, D, FF), D ** -0.5, 0.125, ((0, 8), (2, 4)))
    w_down = noise(key_list[6], (EXPERTS, FF, D), FF ** -0.5, 0.1875, ((0, 8), (1, 4)))
    query_in = noise(key_list[7], (TOKENS, D), 1.0, 6.0, ((0, 8), (1, 4)), jnp.float32)
    key_in = noise(key_list[8], (TOKENS, D), 1.0, 6.0, ((0, 8), (1, 4)), jnp.float32)
    value_in = noise(key_list[9], (TOKENS, D), 1.0, 6.0, ((0, 8), (1, 4)), jnp.float32)
    state_before = noise(key_list[10], (HEADS, HD, HD), (TOKENS ** 0.5), 192.0, ((0, 4),), jnp.float32)
    grad_after = noise(key_list[11], (HEADS, HD, HD), (TOKENS ** 0.5), 192.0, ((0, 4),), jnp.float32)
    return {"hidden_in": hidden_in, "out_grad": out_grad, "expert_ids": expert_ids, "route_weights": route_weights, "w_gate": w_gate, "w_up": w_up, "w_down": w_down, "query_in": query_in, "key_in": key_in, "value_in": value_in, "state_before": state_before, "grad_after": grad_after}


HIGHEST = lax.Precision.HIGHEST


def attention_backward(query_in, key_in, value_in, attn_grad, prefix, suffix, attn_scale):
    block_len = query_in.shape[0]
    causal = jnp.arange(block_len)[:, None] >= jnp.arange(block_len)[None, :]
    score_grad = jnp.einsum("thj,shj->hts", attn_grad, value_in, precision=HIGHEST)
    score_grad = jnp.where(causal[None], score_grad, 0.0)
    score_match = jnp.einsum("thi,shi->hts", query_in, key_in, precision=HIGHEST)
    score_match = jnp.where(causal[None], score_match, 0.0)
    grad_query = jnp.einsum("hts,shi->thi", score_grad, key_in, precision=HIGHEST)
    grad_query = grad_query + jnp.einsum("thj,hij->thi", attn_grad, prefix, precision=HIGHEST)
    grad_key = jnp.einsum("hts,thi->shi", score_grad, query_in, precision=HIGHEST)
    grad_key = grad_key + jnp.einsum("shj,hij->shi", value_in, suffix, precision=HIGHEST)
    grad_value = jnp.einsum("hts,thj->shj", score_match, attn_grad, precision=HIGHEST)
    grad_value = grad_value + jnp.einsum("shi,hij->shj", key_in, suffix, precision=HIGHEST)
    return grad_query * attn_scale, grad_key * attn_scale, grad_value * attn_scale


def expert_reference(row_data, grad_rows, gate_mat, up_mat, down_mat):
    row_wide = row_data.astype(jnp.float32)
    grad_wide = grad_rows.astype(jnp.float32)
    gate_wide = gate_mat.astype(jnp.float32)
    up_wide = up_mat.astype(jnp.float32)
    down_wide = down_mat.astype(jnp.float32)
    pre_gate = jnp.dot(row_wide, gate_wide, precision=HIGHEST)
    pre_up = jnp.dot(row_wide, up_wide, precision=HIGHEST)
    gate_sigmoid = jax.nn.sigmoid(pre_gate)
    gate_swish = pre_gate * gate_sigmoid
    hidden_act = (gate_swish * pre_up).astype(jnp.bfloat16)
    d_inner = jnp.dot(grad_wide, down_wide.T, precision=HIGHEST)
    d_gate = (d_inner * pre_up * gate_sigmoid * (1.0 + pre_gate * (1.0 - gate_sigmoid))).astype(jnp.bfloat16)
    d_up = (d_inner * gate_swish).astype(jnp.bfloat16)
    grad_down = jnp.dot(hidden_act.astype(jnp.float32).T, grad_wide, precision=HIGHEST)
    grad_gate = jnp.dot(row_wide.T, d_gate.astype(jnp.float32), precision=HIGHEST)
    grad_up = jnp.dot(row_wide.T, d_up.astype(jnp.float32), precision=HIGHEST)
    group_width = FF // N_HEAD
    gate_split = gate_wide.reshape(D, N_HEAD, group_width)
    up_split = up_wide.reshape(D, N_HEAD, group_width)
    dgate_split = d_gate.astype(jnp.float32).reshape(-1, N_HEAD, group_width)
    dup_split = d_up.astype(jnp.float32).reshape(-1, N_HEAD, group_width)
    group_part = jnp.einsum("rqf,dqf->qrd", dgate_split, gate_split, precision=HIGHEST)
    group_part = group_part + jnp.einsum("rqf,dqf->qrd", dup_split, up_split, precision=HIGHEST)
    group_round = lax.optimization_barrier(group_part.astype(jnp.bfloat16))
    hidden_part = jnp.sum(group_round.astype(jnp.float32), axis=0)
    return grad_gate.astype(jnp.bfloat16), grad_up.astype(jnp.bfloat16), grad_down.astype(jnp.bfloat16), hidden_part


def reference(hidden_in, out_grad, expert_ids, route_weights, w_gate, w_up, w_down, query_in, key_in, value_in, state_before, grad_after):
    slot_total = N_SEQ * CAP
    flat_ids = expert_ids.reshape(-1)
    onehot = (flat_ids[:, None] == jnp.arange(EXPERTS, dtype=jnp.int32)[None, :]).astype(jnp.int32)
    slot_rank = jnp.sum((jnp.cumsum(onehot, axis=0) - onehot) * onehot, axis=1)
    slot_dest = flat_ids * slot_total + slot_rank
    pair_token = jnp.arange(TOKENS * TOPK, dtype=jnp.int32) // TOPK
    slot_token = jnp.zeros((EXPERTS * slot_total,), jnp.int32).at[slot_dest].set(pair_token)
    slot_weight = jnp.zeros((EXPERTS * slot_total,), jnp.float32).at[slot_dest].set(route_weights.reshape(-1))
    slot_token = slot_token.reshape(EXPERTS, slot_total)
    slot_weight = slot_weight.reshape(EXPERTS, slot_total)

    def one_expert(running_sum, inputs):
        token_ids, pair_weight, gate_mat, up_mat, down_mat = inputs
        row_data = hidden_in[token_ids]
        grad_rows = (pair_weight[:, None] * out_grad[token_ids]).astype(jnp.bfloat16)
        grad_gate, grad_up, grad_down, hidden_part = expert_reference(row_data, grad_rows, gate_mat, up_mat, down_mat)
        running_sum = running_sum.at[token_ids].add(hidden_part)
        return running_sum, (grad_gate, grad_up, grad_down)

    moe_grad, weight_grads = lax.scan(one_expert, jnp.zeros((TOKENS, D), jnp.float32), (slot_token, slot_weight, w_gate, w_up, w_down))
    grad_gate, grad_up, grad_down = weight_grads

    attn_grad = out_grad + moe_grad
    shape_four = (N_SEQ, TOK_DEV, HEADS, HD)
    query_blocks = query_in.reshape(shape_four)
    key_blocks = key_in.reshape(shape_four)
    value_blocks = value_in.reshape(shape_four)
    grad_blocks = attn_grad.reshape(shape_four)
    kv_local = jnp.einsum("cshi,cshj->chij", key_blocks, value_blocks, precision=HIGHEST)
    qd_local = jnp.einsum("cthi,cthj->chij", query_blocks, grad_blocks, precision=HIGHEST)
    zero_state = jnp.zeros((1, HEADS, HD, HD), jnp.float32)
    prefix = jnp.concatenate([zero_state, jnp.cumsum(kv_local, axis=0)[:-1]], axis=0) + state_before[None]
    later_sum = jnp.cumsum(qd_local[::-1], axis=0)[::-1]
    suffix = jnp.concatenate([later_sum[1:], zero_state], axis=0) + grad_after[None]
    attn_scale = (HD * TOKENS) ** -0.5
    grad_query, grad_key, grad_value = jax.vmap(attention_backward, in_axes=(0, 0, 0, 0, 0, 0, None))(
        query_blocks, key_blocks, value_blocks, grad_blocks, prefix, suffix, attn_scale)
    return (grad_gate, grad_up, grad_down, grad_query.reshape(TOKENS, D), grad_key.reshape(TOKENS, D), grad_value.reshape(TOKENS, D))
```

```python
import jax
import jax.numpy as jnp
from jax import lax
from jax.experimental import pallas as pl
from jax.experimental.pallas import tpu as pltpu
from jax.sharding import PartitionSpec as P

EXPERTS = 64
TOPK = 8
HD = 128
CAP = 32


HIGHEST = lax.Precision.HIGHEST


def carried_in(shard, axis, backward):
    place = lax.axis_index(axis)
    gathered = lax.all_gather(shard.astype(jnp.bfloat16), axis).astype(jnp.float32)
    order = jnp.arange(gathered.shape[0])
    used = (order > place) if backward else (order < place)
    return jnp.sum(jnp.where(used[:, None, None, None], gathered, 0.0), axis=0)


def attention_backward(query_in, key_in, value_in, attn_grad, prefix, suffix, attn_scale):
    block_len = query_in.shape[0]
    causal = jnp.arange(block_len)[:, None] >= jnp.arange(block_len)[None, :]
    score_grad = jnp.einsum("thj,shj->hts", attn_grad, value_in, precision=HIGHEST)
    score_grad = jnp.where(causal[None], score_grad, 0.0)
    score_match = jnp.einsum("thi,shi->hts", query_in, key_in, precision=HIGHEST)
    score_match = jnp.where(causal[None], score_match, 0.0)
    grad_query = jnp.einsum("hts,shi->thi", score_grad, key_in, precision=HIGHEST)
    grad_query = grad_query + jnp.einsum("thj,hij->thi", attn_grad, prefix, precision=HIGHEST)
    grad_key = jnp.einsum("hts,thi->shi", score_grad, query_in, precision=HIGHEST)
    grad_key = grad_key + jnp.einsum("shj,hij->shi", value_in, suffix, precision=HIGHEST)
    grad_value = jnp.einsum("hts,thj->shj", score_match, attn_grad, precision=HIGHEST)
    grad_value = grad_value + jnp.einsum("shi,hij->shj", key_in, suffix, precision=HIGHEST)
    return (grad_query * attn_scale, grad_key * attn_scale, grad_value * attn_scale)


NT = (((1,), (1,)), ((), ()))
TN = (((0,), (0,)), ((), ()))


def dot(a, b, dims=(((1,), (0,)), ((), ()))):
    return lax.dot_general(a, b, dims, preferred_element_type=jnp.float32)


def expert_kernel(
    seq_count,
    exp_local,
    x_ref,
    wg_ref,
    wu_ref,
    wd_ref,
    gg_ref,
    gu_ref,
    gd_ref,
    part_ref,
    rows,
    grads,
    picks,
    route,
):
    step = pl.program_id(0)
    heads, tok_rows, _ = x_ref.shape
    feat = part_ref.shape[3]

    @pl.when(step < seq_count)
    def _gather():
        base = lax.axis_index("seq") * exp_local
        route[...] = x_ref[0, :, 2 * feat :].astype(jnp.float32)
        ranks = lax.broadcasted_iota(jnp.int32, (CAP, tok_rows), 0).astype(jnp.float32)
        ones, scaled = [], []
        for e in range(exp_local):
            rank_row = route[pl.ds(base + e, 1), :]
            weight_row = route[pl.ds(EXPERTS + base + e, 1), :]
            hit = ranks == rank_row
            ones.append(jnp.where(hit, 1.0, 0.0))
            scaled.append(jnp.where(hit, weight_row, 0.0))
        one = jnp.concatenate(ones, axis=0).astype(jnp.bfloat16)
        weighted = jnp.concatenate(scaled, axis=0).astype(jnp.bfloat16)
        picks[step] = one
        at = pl.ds(pl.multiple_of(step * CAP, CAP), CAP)
        for h in range(heads):
            cols = pl.ds(h * feat, feat)
            got = dot(one, x_ref[h, :, :feat]).astype(jnp.bfloat16)
            rows[:, at, cols] = got.reshape(exp_local, CAP, feat)
            got = dot(weighted, x_ref[h, :, feat : 2 * feat]).astype(jnp.bfloat16)
            grads[:, at, cols] = got.reshape(exp_local, CAP, feat)

    @pl.when((step >= seq_count) & (step < seq_count + exp_local))
    def _expert():
        e = step - seq_count
        xr = rows[e]
        gr = grads[e]
        wg = wg_ref[0]
        wu = wu_ref[0]
        pre_gate = dot(xr, wg)
        pre_up = dot(xr, wu)
        d_inner = dot(gr, wd_ref[0], NT)
        sig = jax.nn.sigmoid(pre_gate)
        swish = pre_gate * sig
        act = (swish * pre_up).astype(jnp.bfloat16)
        d_gate = (d_inner * pre_up * sig * (1.0 + pre_gate * (1.0 - sig))).astype(jnp.bfloat16)
        d_up = (d_inner * swish).astype(jnp.bfloat16)
        gd_ref[0] = dot(act, gr, TN).astype(jnp.bfloat16)
        gg_ref[0] = dot(xr, d_gate, TN).astype(jnp.bfloat16)
        gu_ref[0] = dot(xr, d_up, TN).astype(jnp.bfloat16)
        rows[e] = (dot(d_gate, wg, NT) + dot(d_up, wu, NT)).astype(jnp.bfloat16)

    @pl.when(step >= seq_count + exp_local)
    def _combine():
        b = step - seq_count - exp_local
        at = pl.ds(pl.multiple_of(b * CAP, CAP), CAP)
        for h in range(heads):
            back = rows[:, at, pl.ds(h * feat, feat)].reshape(exp_local * CAP, feat)
            part_ref[0, h] = dot(picks[b], back, TN).astype(jnp.bfloat16)


def expert_call(x_all, w_gate, w_up, w_down):
    seq_count, heads, tok_rows, width = x_all.shape
    exp_local, model, hidden = w_gate.shape
    feat = model // heads
    slots = seq_count * CAP

    def expert_at(i):
        return (jnp.clip(i - seq_count, 0, exp_local - 1), 0, 0)

    def block_in(i):
        return (jnp.minimum(i, seq_count - 1), 0, 0, 0)

    def block_out(i):
        return (jnp.maximum(i - seq_count - exp_local, 0), 0, 0, 0)

    tall = pl.BlockSpec((1, model, hidden), expert_at)
    flat = pl.BlockSpec((1, hidden, model), expert_at)
    return pl.pallas_call(
        lambda *refs: expert_kernel(seq_count, exp_local, *refs),
        grid=(2 * seq_count + exp_local,),
        in_specs=[pl.BlockSpec((None, heads, tok_rows, width), block_in), tall, tall, flat],
        out_specs=[tall, tall, flat, pl.BlockSpec((1, heads, tok_rows, feat), block_out)],
        out_shape=[
            jax.ShapeDtypeStruct(w_gate.shape, jnp.bfloat16),
            jax.ShapeDtypeStruct(w_up.shape, jnp.bfloat16),
            jax.ShapeDtypeStruct(w_down.shape, jnp.bfloat16),
            jax.ShapeDtypeStruct((seq_count, heads, tok_rows, feat), jnp.bfloat16),
        ],
        scratch_shapes=[
            pltpu.VMEM((exp_local, slots, model), jnp.bfloat16),
            pltpu.VMEM((exp_local, slots, model), jnp.bfloat16),
            pltpu.VMEM((seq_count, exp_local * CAP, tok_rows), jnp.bfloat16),
            pltpu.VMEM((2 * EXPERTS, tok_rows), jnp.float32),
        ],
        compiler_params=pltpu.CompilerParams(vmem_limit_bytes=56 * 1024 * 1024),
        cost_estimate=pl.CostEstimate(
            flops=16 * exp_local * slots * model * hidden,
            bytes_accessed=12 * exp_local * model * hidden,
            transcendentals=0,
        ),
    )(x_all, w_gate, w_up, w_down)


def route_table(expert_ids, route_weights):
    tok_rows = expert_ids.shape[0]
    named = (expert_ids.T[:, None, :] == jnp.arange(EXPERTS, dtype=jnp.int32)[None, :, None])
    mask = jnp.any(named, axis=0)
    weight = jnp.sum(jnp.where(named, route_weights.T[:, None, :], 0.0), axis=0)
    before = jnp.arange(tok_rows)[:, None] < jnp.arange(tok_rows)[None, :]
    rank = jnp.dot(
        mask.astype(jnp.bfloat16), before.astype(jnp.bfloat16), preferred_element_type=jnp.float32
    )
    rank = jnp.where(mask, rank, -1.0)
    return jnp.concatenate([rank, weight], axis=0).astype(jnp.bfloat16)


def per_device(
    hidden_in,
    out_grad,
    expert_ids,
    route_weights,
    w_gate,
    w_up,
    w_down,
    query_in,
    key_in,
    value_in,
    state_before,
    grad_after,
):
    seq_count = lax.axis_size("seq")
    heads = lax.axis_size("head")
    tok_rows = expert_ids.shape[0]
    head_local = query_in.shape[1] // HD
    sent = jnp.concatenate(
        [
            hidden_in,
            out_grad.astype(jnp.bfloat16),
            route_table(expert_ids, route_weights),
        ],
        axis=1,
    )
    x_all = lax.all_gather(sent, ("seq", "head"))
    x_all = x_all.reshape(seq_count, heads, tok_rows, sent.shape[1])
    query_heads = query_in.reshape(tok_rows, head_local, HD)
    key_heads = key_in.reshape(tok_rows, head_local, HD)
    value_heads = value_in.reshape(tok_rows, head_local, HD)
    kv_local = jnp.einsum("shi,shj->hij", key_heads, value_heads, precision=HIGHEST)
    prefix = carried_in(kv_local, "seq", False) + state_before
    grad_gate, grad_up, grad_down, part = expert_call(x_all, w_gate, w_up, w_down)
    part = part.reshape(seq_count * heads, tok_rows, -1)
    moe_grad = lax.psum_scatter(part, ("seq", "head"), scatter_dimension=0, tiled=True)
    moe_grad = moe_grad.reshape(tok_rows, -1).astype(jnp.float32)
    attn_grad = (out_grad + moe_grad).reshape(tok_rows, head_local, HD)
    qd_local = jnp.einsum("thi,thj->hij", query_heads, attn_grad, precision=HIGHEST)
    suffix = carried_in(qd_local, "seq", True) + grad_after
    attn_scale = (HD * tok_rows * seq_count) ** (-0.5)
    grad_query, grad_key, grad_value = attention_backward(
        query_heads, key_heads, value_heads, attn_grad, prefix, suffix, attn_scale
    )
    return (
        grad_gate,
        grad_up,
        grad_down,
        grad_query.reshape(tok_rows, -1),
        grad_key.reshape(tok_rows, -1),
        grad_value.reshape(tok_rows, -1),
    )


def solution(mesh):
    placed = (
        P("seq", "head"),
        P("seq", "head"),
        P("seq", None),
        P("seq", None),
        P("seq", None, "head"),
        P("seq", None, "head"),
        P("seq", "head", None),
        P("seq", "head"),
        P("seq", "head"),
        P("seq", "head"),
        P("head", None, None),
        P("head", None, None),
    )
    return jax.shard_map(
        per_device,
        mesh=mesh,
        in_specs=placed,
        out_specs=(
            P("seq", None, "head"),
            P("seq", None, "head"),
            P("seq", "head", None),
            P("seq", "head"),
            P("seq", "head"),
            P("seq", "head"),
        ),
        check_vma=False,
    )
```

```python
import jax
import jax.numpy as jnp
from jax import lax
from jax.experimental import pallas as pl
from jax.experimental.pallas import tpu as pltpu
from jax.sharding import PartitionSpec as P

EXPERTS = 64
TOPK = 8
HD = 128
CAP = 32


HIGHEST = lax.Precision.HIGHEST
MESH = pl.DeviceIdType.MESH


def carried_in(shard, axis, backward):
    place = lax.axis_index(axis)
    gathered = lax.all_gather(shard.astype(jnp.bfloat16), axis).astype(jnp.float32)
    order = jnp.arange(gathered.shape[0])
    used = (order > place) if backward else (order < place)
    return jnp.sum(jnp.where(used[:, None, None, None], gathered, 0.0), axis=0)


def attention_backward(query_in, key_in, value_in, attn_grad, prefix, suffix, attn_scale):
    block_len = query_in.shape[0]
    causal = jnp.arange(block_len)[:, None] >= jnp.arange(block_len)[None, :]
    score_grad = jnp.einsum("thj,shj->hts", attn_grad, value_in, precision=HIGHEST)
    score_grad = jnp.where(causal[None], score_grad, 0.0)
    score_match = jnp.einsum("thi,shi->hts", query_in, key_in, precision=HIGHEST)
    score_match = jnp.where(causal[None], score_match, 0.0)
    grad_query = jnp.einsum("hts,shi->thi", score_grad, key_in, precision=HIGHEST)
    grad_query = grad_query + jnp.einsum("thj,hij->thi", attn_grad, prefix, precision=HIGHEST)
    grad_key = jnp.einsum("hts,thi->shi", score_grad, query_in, precision=HIGHEST)
    grad_key = grad_key + jnp.einsum("shj,hij->shi", value_in, suffix, precision=HIGHEST)
    grad_value = jnp.einsum("hts,thj->shj", score_match, attn_grad, precision=HIGHEST)
    grad_value = grad_value + jnp.einsum("shi,hij->shj", key_in, suffix, precision=HIGHEST)
    return (grad_query * attn_scale, grad_key * attn_scale, grad_value * attn_scale)


NT = (((1,), (1,)), ((), ()))
TN = (((0,), (0,)), ((), ()))


def dot(a, b, dims=(((1,), (0,)), ((), ()))):
    return lax.dot_general(a, b, dims, preferred_element_type=jnp.float32)


def expert_kernel(
    seq_count,
    exp_local,
    x_ref,
    wg_ref,
    wu_ref,
    wd_ref,
    gg_ref,
    gu_ref,
    gd_ref,
    part_ref,
    rows,
    grads,
    picks,
    route,
):
    step = pl.program_id(0)
    heads, tok_rows, _ = x_ref.shape
    feat = part_ref.shape[3]

    @pl.when(step < seq_count)
    def _gather():
        base = lax.axis_index("seq") * exp_local
        route[...] = x_ref[0, :, 2 * feat :].astype(jnp.float32)
        ranks = lax.broadcasted_iota(jnp.int32, (CAP, tok_rows), 0).astype(jnp.float32)
        ones, scaled = [], []
        for e in range(exp_local):
            rank_row = route[pl.ds(base + e, 1), :]
            weight_row = route[pl.ds(EXPERTS + base + e, 1), :]
            hit = ranks == rank_row
            ones.append(jnp.where(hit, 1.0, 0.0))
            scaled.append(jnp.where(hit, weight_row, 0.0))
        one = jnp.concatenate(ones, axis=0).astype(jnp.bfloat16)
        weighted = jnp.concatenate(scaled, axis=0).astype(jnp.bfloat16)
        picks[step] = one
        at = pl.ds(pl.multiple_of(step * CAP, CAP), CAP)
        for h in range(heads):
            cols = pl.ds(h * feat, feat)
            got = dot(one, x_ref[h, :, :feat]).astype(jnp.bfloat16)
            rows[:, at, cols] = got.reshape(exp_local, CAP, feat)
            got = dot(weighted, x_ref[h, :, feat : 2 * feat]).astype(jnp.bfloat16)
            grads[:, at, cols] = got.reshape(exp_local, CAP, feat)

    @pl.when((step >= seq_count) & (step < seq_count + exp_local))
    def _expert():
        e = step - seq_count
        xr = rows[e]
        gr = grads[e]
        wg = wg_ref[0]
        wu = wu_ref[0]
        pre_gate = dot(xr, wg)
        pre_up = dot(xr, wu)
        d_inner = dot(gr, wd_ref[0], NT)
        sig = jax.nn.sigmoid(pre_gate)
        swish = pre_gate * sig
        act = (swish * pre_up).astype(jnp.bfloat16)
        d_gate = (d_inner * pre_up * sig * (1.0 + pre_gate * (1.0 - sig))).astype(jnp.bfloat16)
        d_up = (d_inner * swish).astype(jnp.bfloat16)
        gd_ref[0] = dot(act, gr, TN).astype(jnp.bfloat16)
        gg_ref[0] = dot(xr, d_gate, TN).astype(jnp.bfloat16)
        gu_ref[0] = dot(xr, d_up, TN).astype(jnp.bfloat16)
        rows[e] = (dot(d_gate, wg, NT) + dot(d_up, wu, NT)).astype(jnp.bfloat16)

    @pl.when(step >= seq_count + exp_local)
    def _combine():
        b = step - seq_count - exp_local
        at = pl.ds(pl.multiple_of(b * CAP, CAP), CAP)
        for h in range(heads):
            back = rows[:, at, pl.ds(h * feat, feat)].reshape(exp_local * CAP, feat)
            part_ref[0, h] = dot(picks[b], back, TN).astype(jnp.bfloat16)


def expert_call(x_all, w_gate, w_up, w_down):
    seq_count, heads, tok_rows, width = x_all.shape
    exp_local, model, hidden = w_gate.shape
    feat = model // heads
    slots = seq_count * CAP

    def expert_at(i):
        return (jnp.clip(i - seq_count, 0, exp_local - 1), 0, 0)

    def block_in(i):
        return (jnp.minimum(i, seq_count - 1), 0, 0, 0)

    def block_out(i):
        return (jnp.maximum(i - seq_count - exp_local, 0), 0, 0, 0)

    tall = pl.BlockSpec((1, model, hidden), expert_at)
    flat = pl.BlockSpec((1, hidden, model), expert_at)
    return pl.pallas_call(
        lambda *refs: expert_kernel(seq_count, exp_local, *refs),
        grid=(2 * seq_count + exp_local,),
        in_specs=[pl.BlockSpec((None, heads, tok_rows, width), block_in), tall, tall, flat],
        out_specs=[tall, tall, flat, pl.BlockSpec((1, heads, tok_rows, feat), block_out)],
        out_shape=[
            jax.ShapeDtypeStruct(w_gate.shape, jnp.bfloat16),
            jax.ShapeDtypeStruct(w_up.shape, jnp.bfloat16),
            jax.ShapeDtypeStruct(w_down.shape, jnp.bfloat16),
            jax.ShapeDtypeStruct((seq_count, heads, tok_rows, feat), jnp.bfloat16),
        ],
        scratch_shapes=[
            pltpu.VMEM((exp_local, slots, model), jnp.bfloat16),
            pltpu.VMEM((exp_local, slots, model), jnp.bfloat16),
            pltpu.VMEM((seq_count, exp_local * CAP, tok_rows), jnp.bfloat16),
            pltpu.VMEM((2 * EXPERTS, tok_rows), jnp.float32),
        ],
        compiler_params=pltpu.CompilerParams(vmem_limit_bytes=56 * 1024 * 1024),
        cost_estimate=pl.CostEstimate(
            flops=16 * exp_local * slots * model * hidden,
            bytes_accessed=12 * exp_local * model * hidden,
            transcendentals=0,
        ),
    )(x_all, w_gate, w_up, w_down)


def place_of(depth):
    s, h = lax.axis_index("seq"), lax.axis_index("head")
    return s // 2, s % 2, h // 2, h % 2


def device_of(z, x, y, c):
    return (z * 2 + x, y * 2 + c)


def partners_of(z, x, y, c):
    other_x, other_y = 1 - x, 1 - y
    sibling = device_of(z, x, y, 1 - c)
    first = device_of(z, c * other_x + (1 - c) * x, (1 - c) * other_y + c * y, c)
    second = device_of(z, (1 - c) * other_x + c * x, c * other_y + (1 - c) * y, c)
    return sibling, first, second


def greet(depth, z, x, y, c):
    barrier = pltpu.get_barrier_semaphore()
    known = list(partners_of(z, x, y, c))
    known += [device_of((z + k) % depth, x, y, c) for k in range(1, depth)]
    for device in known:
        pl.semaphore_signal(barrier, inc=1, device_id=device, device_id_type=MESH)
    pl.semaphore_wait(barrier, len(known))


def send(source, target, send_sem, recv_sem, device):
    copy = pltpu.make_async_remote_copy(
        src_ref=source,
        dst_ref=target,
        send_sem=send_sem,
        recv_sem=recv_sem,
        device_id=device,
        device_id_type=MESH,
    )
    copy.start()
    return copy


def spread_kernel(depth, own_ref, all_ref, local_sem, z_send, z_recv, p_send, p_recv):
    z, x, y, c = place_of(depth)
    sibling, first, second = partners_of(z, x, y, c)
    mine_a = (1 - c) * y + c * x
    mine_b = c * y + (1 - c) * x

    def slot(zi, a, b):
        return all_ref.at[zi, c * a + (1 - c) * b, (1 - c) * a + c * b, c]

    greet(depth, z, x, y, c)
    local = pltpu.make_async_copy(own_ref, slot(z, mine_a, mine_b), local_sem)
    local.start()
    along = [None] * depth
    for k in range(1, depth):
        along[k] = send(
            own_ref,
            slot(z, mine_a, mine_b),
            z_send.at[k],
            z_recv.at[k],
            device_of((z + k) % depth, x, y, c),
        )
    sent = {}

    def start(kind, k, source, target, device):
        at = kind * depth + k
        sent[kind, k] = send(source, target, p_send.at[at], p_recv.at[at], device)

    def arrive_z(k):
        target = slot((z + depth - k) % depth, mine_a, mine_b)
        if k:
            along[k].wait_recv()
        source = target if k else own_ref
        start(0, k, source, target, first)
        start(1, k, source, target, second)
        start(3, k, source, target, sibling)

    def arrive_first(k):
        sent[0, k].wait_recv()
        target = slot((z + depth - k) % depth, 1 - mine_a, mine_b)
        start(2, k, target, target, second)
        start(4, k, target, target, sibling)

    for t in range(depth + 1):
        if t < depth:
            arrive_z(t)
        if t:
            arrive_first(t - 1)
    for kind, a in ((1, mine_a), (2, 1 - mine_a)):
        for k in range(depth):
            sent[kind, k].wait_recv()
            target = slot((z + depth - k) % depth, a, 1 - mine_b)
            start(kind + 4, k, target, target, sibling)
    for kind in (3, 4, 5, 6):
        for k in range(depth):
            sent[kind, k].wait_recv()
    for k in range(1, depth):
        along[k].wait_send()
    for copy in sent.values():
        copy.wait_send()
    local.wait()


def spread(own, seq_count, heads):
    depth = seq_count // 2
    shape = (depth, 2, 2, 2) + own.shape
    everything = pl.pallas_call(
        lambda *refs: spread_kernel(depth, *refs),
        out_shape=jax.ShapeDtypeStruct(shape, own.dtype),
        in_specs=[pl.BlockSpec(memory_space=pl.ANY)],
        out_specs=pl.BlockSpec(memory_space=pl.ANY),
        scratch_shapes=[
            pltpu.SemaphoreType.DMA,
            pltpu.SemaphoreType.DMA((depth,)),
            pltpu.SemaphoreType.DMA((depth,)),
            pltpu.SemaphoreType.DMA((7 * depth,)),
            pltpu.SemaphoreType.DMA((7 * depth,)),
        ],
        compiler_params=pltpu.CompilerParams(collective_id=0, has_side_effects=True),
        cost_estimate=pl.CostEstimate(flops=0, bytes_accessed=1 << 26, transcendentals=0),
    )(own)
    return everything.reshape((seq_count, heads) + own.shape)


def collect_kernel(
    depth,
    part_ref,
    out_grad_ref,
    query_ref,
    grad_ref,
    later_ref,
    core_got,
    one,
    one_got,
    two,
    two_got,
    three,
    three_got,
    state_out,
    state_x,
    pair_out,
    pair_got,
    send_sems,
    recv_sems,
    state_send,
    state_recv,
):
    z, x, y, c = place_of(depth)
    sibling, first, second = partners_of(z, x, y, c)
    mine_a = (1 - c) * y + c * x
    mine_b = c * y + (1 - c) * x
    greet(depth, z, x, y, c)
    copies = []
    order = list(range(1, depth)) + [0]

    def start(kind, k, source, target, device):
        at = kind * depth + k
        copy = send(source, target, send_sems.at[at], recv_sems.at[at], device)
        copies.append(copy)
        return copy

    core, step_a, step_b, step_z = {}, {}, {}, {}
    for k in order:
        zi = (z + k) % depth
        core[k] = start(0, k, part_ref.at[zi, :, :, 1 - c], core_got.at[k], sibling)
    for k in order:
        zi = (z + k) % depth
        core[k].wait_recv()
        for a in range(2):
            for b in range(2):
                at_x, at_y = c * a + (1 - c) * b, (1 - c) * a + c * b
                total = part_ref[zi, at_x, at_y, c].astype(jnp.float32)
                total = total + core_got[k, at_x, at_y].astype(jnp.float32)
                one[k, a, b] = total.astype(jnp.bfloat16)
        step_a[k] = start(1, k, one.at[k, 1 - mine_a], one_got.at[k], first)
    for k in order:
        step_a[k].wait_recv()
        total = one[k, mine_a].astype(jnp.float32) + one_got[k].astype(jnp.float32)
        two[k] = total.astype(jnp.bfloat16)
        step_b[k] = start(2, k, two.at[k, 1 - mine_b], two_got.at[k], second)
    for k in order:
        step_b[k].wait_recv()
        total = two[k, mine_b].astype(jnp.float32) + two_got[k].astype(jnp.float32)
        if k:
            three[k] = total.astype(jnp.bfloat16)
            device = device_of((z + k) % depth, x, y, c)
            step_z[k] = start(3, k, three.at[k], three_got.at[k], device)
        else:
            grad_ref[...] = out_grad_ref[...] + total
    for k in range(1, depth):
        step_z[k].wait_recv()
        grad_ref[...] += three_got[k].astype(jnp.float32)

    heads = later_ref.shape[0]
    for h in range(heads):
        cols = pl.ds(h * HD, HD)
        later_ref[h] = lax.dot_general(
            query_ref[:, cols],
            grad_ref[:, cols],
            TN,
            precision=HIGHEST,
            preferred_element_type=jnp.float32,
        )
    state_out[...] = later_ref[...].astype(jnp.bfloat16)
    swap = send(
        state_out,
        state_x,
        state_send.at[0],
        state_recv.at[0],
        device_of(z, 1 - x, y, c),
    )
    copies.append(swap)
    swap.wait_recv()
    got = state_x[...].astype(jnp.float32)
    pair_out[...] = (later_ref[...] + got).astype(jnp.bfloat16)
    shared = []
    for k in range(1, depth):
        device = device_of((z + k) % depth, x, y, c)
        shared.append(
            send(pair_out, pair_got.at[k], state_send.at[k], state_recv.at[k], device)
        )
    later_ref[...] = got * (1 - x).astype(jnp.float32)
    for k in range(1, depth):
        shared[k - 1].wait_recv()
        counted = ((z + depth - k) % depth > z).astype(jnp.float32)
        later_ref[...] += pair_got[k].astype(jnp.float32) * counted
    for copy in copies + shared:
        copy.wait_send()


def collect(part, out_grad, query_in):
    seq_count, heads, rows, feat = part.shape
    depth = seq_count // 2
    part = part.reshape(depth, 2, 2, 2, rows, feat)
    state = (feat // HD, HD, HD)
    kind = jnp.bfloat16
    return pl.pallas_call(
        lambda *refs: collect_kernel(depth, *refs),
        out_shape=[
            jax.ShapeDtypeStruct((rows, feat), jnp.float32),
            jax.ShapeDtypeStruct(state, jnp.float32),
        ],
        in_specs=[pl.BlockSpec(memory_space=pltpu.VMEM)] * 3,
        out_specs=[pl.BlockSpec(memory_space=pltpu.VMEM)] * 2,
        scratch_shapes=[
            pltpu.VMEM((depth, 2, 2, rows, feat), kind),
            pltpu.VMEM((depth, 2, 2, rows, feat), kind),
            pltpu.VMEM((depth, 2, rows, feat), kind),
            pltpu.VMEM((depth, 2, rows, feat), kind),
            pltpu.VMEM((depth, rows, feat), kind),
            pltpu.VMEM((depth, rows, feat), kind),
            pltpu.VMEM((depth, rows, feat), kind),
            pltpu.VMEM(state, kind),
            pltpu.VMEM(state, kind),
            pltpu.VMEM(state, kind),
            pltpu.VMEM((depth,) + state, kind),
            pltpu.SemaphoreType.DMA((4 * depth,)),
            pltpu.SemaphoreType.DMA((4 * depth,)),
            pltpu.SemaphoreType.DMA((depth,)),
            pltpu.SemaphoreType.DMA((depth,)),
        ],
        compiler_params=pltpu.CompilerParams(
            collective_id=1, has_side_effects=True, vmem_limit_bytes=56 * 1024 * 1024
        ),
        cost_estimate=pl.CostEstimate(flops=0, bytes_accessed=1 << 26, transcendentals=0),
    )(part, out_grad, query_in)


def route_table(expert_ids, route_weights):
    tok_rows = expert_ids.shape[0]
    named = (expert_ids.T[:, None, :] == jnp.arange(EXPERTS, dtype=jnp.int32)[None, :, None])
    mask = jnp.any(named, axis=0)
    weight = jnp.sum(jnp.where(named, route_weights.T[:, None, :], 0.0), axis=0)
    before = jnp.arange(tok_rows)[:, None] < jnp.arange(tok_rows)[None, :]
    rank = jnp.dot(
        mask.astype(jnp.bfloat16), before.astype(jnp.bfloat16), preferred_element_type=jnp.float32
    )
    rank = jnp.where(mask, rank, -1.0)
    return jnp.concatenate([rank, weight], axis=0).astype(jnp.bfloat16)


def per_device(
    hidden_in,
    out_grad,
    expert_ids,
    route_weights,
    w_gate,
    w_up,
    w_down,
    query_in,
    key_in,
    value_in,
    state_before,
    grad_after,
):
    seq_count = lax.axis_size("seq")
    heads = lax.axis_size("head")
    tok_rows = expert_ids.shape[0]
    head_local = query_in.shape[1] // HD
    sent = jnp.concatenate(
        [
            hidden_in,
            out_grad.astype(jnp.bfloat16),
            route_table(expert_ids, route_weights),
        ],
        axis=1,
    )
    if heads == 4 and seq_count % 2 == 0:
        x_all = spread(sent, seq_count, heads)
    else:
        x_all = lax.all_gather(sent, ("seq", "head"))
        x_all = x_all.reshape(seq_count, heads, tok_rows, sent.shape[1])
    query_heads = query_in.reshape(tok_rows, head_local, HD)
    key_heads = key_in.reshape(tok_rows, head_local, HD)
    value_heads = value_in.reshape(tok_rows, head_local, HD)
    kv_local = jnp.einsum("shi,shj->hij", key_heads, value_heads, precision=HIGHEST)
    prefix = carried_in(kv_local, "seq", False) + state_before
    grad_gate, grad_up, grad_down, part = expert_call(x_all, w_gate, w_up, w_down)
    if heads == 4 and seq_count % 2 == 0:
        attn_grad, later = collect(part, out_grad, query_in)
        attn_grad = attn_grad.reshape(tok_rows, head_local, HD)
        suffix = later + grad_after
    else:
        part = part.reshape(seq_count * heads, tok_rows, -1)
        moe_grad = lax.psum_scatter(part, ("seq", "head"), scatter_dimension=0, tiled=True)
        moe_grad = moe_grad.reshape(tok_rows, -1).astype(jnp.float32)
        attn_grad = (out_grad + moe_grad).reshape(tok_rows, head_local, HD)
        qd_local = jnp.einsum("thi,thj->hij", query_heads, attn_grad, precision=HIGHEST)
        suffix = carried_in(qd_local, "seq", True) + grad_after
    attn_scale = (HD * tok_rows * seq_count) ** (-0.5)
    grad_query, grad_key, grad_value = attention_backward(
        query_heads, key_heads, value_heads, attn_grad, prefix, suffix, attn_scale
    )
    return (
        grad_gate,
        grad_up,
        grad_down,
        grad_query.reshape(tok_rows, -1),
        grad_key.reshape(tok_rows, -1),
        grad_value.reshape(tok_rows, -1),
    )


def solution(mesh):
    placed = (
        P("seq", "head"),
        P("seq", "head"),
        P("seq", None),
        P("seq", None),
        P("seq", None, "head"),
        P("seq", None, "head"),
        P("seq", "head", None),
        P("seq", "head"),
        P("seq", "head"),
        P("seq", "head"),
        P("head", None, None),
        P("head", None, None),
    )
    return jax.shard_map(
        per_device,
        mesh=mesh,
        in_specs=placed,
        out_specs=(
            P("seq", None, "head"),
            P("seq", None, "head"),
            P("seq", "head", None),
            P("seq", "head"),
            P("seq", "head"),
            P("seq", "head"),
        ),
        check_vma=False,
    )
```

```python
import jax
import jax.numpy as jnp
from jax import lax
from jax.experimental import pallas as pl
from jax.experimental.pallas import tpu as pltpu
from jax.sharding import PartitionSpec as P

EXPERTS = 64
TOPK = 8
HD = 128
CAP = 32


HIGHEST = lax.Precision.HIGHEST
MESH = pl.DeviceIdType.MESH


def carried_in(shard, axis, backward):
    place = lax.axis_index(axis)
    gathered = lax.all_gather(shard.astype(jnp.bfloat16), axis).astype(jnp.float32)
    order = jnp.arange(gathered.shape[0])
    used = (order > place) if backward else (order < place)
    return jnp.sum(jnp.where(used[:, None, None, None], gathered, 0.0), axis=0)


def attention_backward(query_in, key_in, value_in, attn_grad, prefix, suffix, attn_scale):
    block_len = query_in.shape[0]
    causal = jnp.arange(block_len)[:, None] >= jnp.arange(block_len)[None, :]
    score_grad = jnp.einsum("thj,shj->hts", attn_grad, value_in, precision=HIGHEST)
    score_grad = jnp.where(causal[None], score_grad, 0.0)
    score_match = jnp.einsum("thi,shi->hts", query_in, key_in, precision=HIGHEST)
    score_match = jnp.where(causal[None], score_match, 0.0)
    grad_query = jnp.einsum("hts,shi->thi", score_grad, key_in, precision=HIGHEST)
    grad_query = grad_query + jnp.einsum("thj,hij->thi", attn_grad, prefix, precision=HIGHEST)
    grad_key = jnp.einsum("hts,thi->shi", score_grad, query_in, precision=HIGHEST)
    grad_key = grad_key + jnp.einsum("shj,hij->shi", value_in, suffix, precision=HIGHEST)
    grad_value = jnp.einsum("hts,thj->shj", score_match, attn_grad, precision=HIGHEST)
    grad_value = grad_value + jnp.einsum("shi,hij->shj", key_in, suffix, precision=HIGHEST)
    return (grad_query * attn_scale, grad_key * attn_scale, grad_value * attn_scale)


NN = (((1,), (0,)), ((), ()))
NT = (((1,), (1,)), ((), ()))
TN = (((0,), (0,)), ((), ()))


def dot(a, b, dims=NN):
    return lax.dot_general(a, b, dims, preferred_element_type=jnp.float32)


def expert_kernel(
    seq_count,
    exp_local,
    x_ref,
    wg_ref,
    wu_ref,
    wd_ref,
    gg_ref,
    gu_ref,
    gd_ref,
    part_ref,
    rows,
    grads,
    picks,
    route,
):
    step = pl.program_id(0)
    heads, tok_rows, _ = x_ref.shape
    feat = part_ref.shape[3]

    @pl.when(step < seq_count)
    def _gather():
        base = lax.axis_index("seq") * exp_local
        route[...] = x_ref[0, :, 2 * feat :].astype(jnp.float32)
        ranks = lax.broadcasted_iota(jnp.int32, (CAP, tok_rows), 0).astype(jnp.float32)
        ones, scaled = [], []
        for e in range(exp_local):
            rank_row = route[pl.ds(base + e, 1), :]
            weight_row = route[pl.ds(EXPERTS + base + e, 1), :]
            hit = ranks == rank_row
            ones.append(jnp.where(hit, 1.0, 0.0))
            scaled.append(jnp.where(hit, weight_row, 0.0))
        one = jnp.concatenate(ones, axis=0).astype(jnp.bfloat16)
        weighted = jnp.concatenate(scaled, axis=0).astype(jnp.bfloat16)
        picks[step] = one
        at = pl.ds(pl.multiple_of(step * CAP, CAP), CAP)
        for h in range(heads):
            cols = pl.ds(h * feat, feat)
            got = dot(one, x_ref[h, :, :feat]).astype(jnp.bfloat16)
            rows[:, at, cols] = got.reshape(exp_local, CAP, feat)
            got = dot(weighted, x_ref[h, :, feat : 2 * feat]).astype(jnp.bfloat16)
            grads[:, at, cols] = got.reshape(exp_local, CAP, feat)

    @pl.when((step >= seq_count) & (step < seq_count + exp_local))
    def _expert():
        e = step - seq_count
        xr = rows[e]
        gr = grads[e]
        wg = wg_ref[0]
        wu = wu_ref[0]
        pre_gate = dot(xr, wg)
        pre_up = dot(xr, wu)
        d_inner = dot(gr, wd_ref[0], NT)
        sig = jax.nn.sigmoid(pre_gate)
        swish = pre_gate * sig
        act = (swish * pre_up).astype(jnp.bfloat16)
        d_gate = (d_inner * pre_up * sig * (1.0 + pre_gate * (1.0 - sig))).astype(jnp.bfloat16)
        d_up = (d_inner * swish).astype(jnp.bfloat16)
        gd_ref[0] = dot(act, gr, TN).astype(jnp.bfloat16)
        gg_ref[0] = dot(xr, d_gate, TN).astype(jnp.bfloat16)
        gu_ref[0] = dot(xr, d_up, TN).astype(jnp.bfloat16)
        rows[e] = (dot(d_gate, wg, NT) + dot(d_up, wu, NT)).astype(jnp.bfloat16)

    @pl.when(step >= seq_count + exp_local)
    def _combine():
        b = step - seq_count - exp_local
        at = pl.ds(pl.multiple_of(b * CAP, CAP), CAP)
        for h in range(heads):
            back = rows[:, at, pl.ds(h * feat, feat)].reshape(exp_local * CAP, feat)
            part_ref[0, h] = dot(picks[b], back, TN).astype(jnp.bfloat16)


def expert_call(x_all, w_gate, w_up, w_down):
    seq_count, heads, tok_rows, width = x_all.shape
    exp_local, model, hidden = w_gate.shape
    feat = model // heads
    slots = seq_count * CAP

    def expert_at(i):
        return (jnp.clip(i - seq_count, 0, exp_local - 1), 0, 0)

    def block_in(i):
        return (jnp.minimum(i, seq_count - 1), 0, 0, 0)

    def block_out(i):
        return (jnp.maximum(i - seq_count - exp_local, 0), 0, 0, 0)

    tall = pl.BlockSpec((1, model, hidden), expert_at)
    flat = pl.BlockSpec((1, hidden, model), expert_at)
    return pl.pallas_call(
        lambda *refs: expert_kernel(seq_count, exp_local, *refs),
        grid=(2 * seq_count + exp_local,),
        in_specs=[pl.BlockSpec((None, heads, tok_rows, width), block_in), tall, tall, flat],
        out_specs=[tall, tall, flat, pl.BlockSpec((1, heads, tok_rows, feat), block_out)],
        out_shape=[
            jax.ShapeDtypeStruct(w_gate.shape, jnp.bfloat16),
            jax.ShapeDtypeStruct(w_up.shape, jnp.bfloat16),
            jax.ShapeDtypeStruct(w_down.shape, jnp.bfloat16),
            jax.ShapeDtypeStruct((seq_count, heads, tok_rows, feat), jnp.bfloat16),
        ],
        scratch_shapes=[
            pltpu.VMEM((exp_local, slots, model), jnp.bfloat16),
            pltpu.VMEM((exp_local, slots, model), jnp.bfloat16),
            pltpu.VMEM((seq_count, exp_local * CAP, tok_rows), jnp.bfloat16),
            pltpu.VMEM((2 * EXPERTS, tok_rows), jnp.float32),
        ],
        compiler_params=pltpu.CompilerParams(vmem_limit_bytes=56 * 1024 * 1024),
        cost_estimate=pl.CostEstimate(
            flops=16 * exp_local * slots * model * hidden,
            bytes_accessed=12 * exp_local * model * hidden,
            transcendentals=0,
        ),
    )(x_all, w_gate, w_up, w_down)


def fine_dot(a, b, dims):
    return lax.dot_general(a, b, dims, precision=HIGHEST, preferred_element_type=jnp.float32)


def place_of(depth):
    s, h = lax.axis_index("seq"), lax.axis_index("head")
    return s // 2, s % 2, h // 2, h % 2


def device_of(z, x, y, c):
    return (z * 2 + x, y * 2 + c)


def turned(depth, z, k, back=False):
    if depth & (depth - 1):
        return (z + (depth - k if back else k)) % depth
    result, bit = 0, 1
    while bit < depth:
        own = (z // bit) % 2
        result = result + bit * (1 - own if k & bit else own)
        bit *= 2
    return result


def partners_of(z, x, y, c):
    other_x, other_y = 1 - x, 1 - y
    sibling = device_of(z, x, y, 1 - c)
    first = device_of(z, c * other_x + (1 - c) * x, (1 - c) * other_y + c * y, c)
    second = device_of(z, (1 - c) * other_x + c * x, c * other_y + (1 - c) * y, c)
    return sibling, first, second


def greet(depth, z, x, y, c):
    barrier = pltpu.get_barrier_semaphore()
    known = list(partners_of(z, x, y, c))
    known += [device_of(turned(depth, z, k), x, y, c) for k in range(1, depth)]
    for device in known:
        pl.semaphore_signal(barrier, inc=1, device_id=device, device_id_type=MESH)
    pl.semaphore_wait(barrier, len(known))


def send(source, target, send_sem, recv_sem, device):
    copy = pltpu.make_async_remote_copy(
        src_ref=source,
        dst_ref=target,
        send_sem=send_sem,
        recv_sem=recv_sem,
        device_id=device,
        device_id_type=MESH,
    )
    copy.start()
    return copy


def spread_kernel(depth, own_ref, all_ref, local_sem, z_send, z_recv, p_send, p_recv):
    z, x, y, c = place_of(depth)
    sibling, first, second = partners_of(z, x, y, c)
    mine_a = (1 - c) * y + c * x
    mine_b = c * y + (1 - c) * x

    def slot(zi, a, b):
        return all_ref.at[zi, c * a + (1 - c) * b, (1 - c) * a + c * b, c]

    greet(depth, z, x, y, c)
    local = pltpu.make_async_copy(own_ref, slot(z, mine_a, mine_b), local_sem)
    local.start()
    along = [None] * depth
    for k in range(1, depth):
        along[k] = send(
            own_ref,
            slot(z, mine_a, mine_b),
            z_send.at[k],
            z_recv.at[k],
            device_of(turned(depth, z, k), x, y, c),
        )
    sent = {}

    def start(kind, k, source, target, device):
        at = kind * depth + k
        sent[kind, k] = send(source, target, p_send.at[at], p_recv.at[at], device)

    def arrive_z(k):
        target = slot(turned(depth, z, k, True), mine_a, mine_b)
        if k:
            along[k].wait_recv()
        source = target if k else own_ref
        start(0, k, source, target, first)
        start(1, k, source, target, second)
        start(3, k, source, target, sibling)

    def arrive_first(k):
        sent[0, k].wait_recv()
        target = slot(turned(depth, z, k, True), 1 - mine_a, mine_b)
        start(2, k, target, target, second)
        start(4, k, target, target, sibling)

    for t in range(depth + 1):
        if t < depth:
            arrive_z(t)
        if t:
            arrive_first(t - 1)
    for kind, a in ((1, mine_a), (2, 1 - mine_a)):
        for k in range(depth):
            sent[kind, k].wait_recv()
            target = slot(turned(depth, z, k, True), a, 1 - mine_b)
            start(kind + 4, k, target, target, sibling)
    for kind in (3, 4, 5, 6):
        for k in range(depth):
            sent[kind, k].wait_recv()
    for k in range(1, depth):
        along[k].wait_send()
    for copy in sent.values():
        copy.wait_send()
    local.wait()


def spread(own, seq_count, heads):
    depth = seq_count // 2
    shape = (depth, 2, 2, 2) + own.shape
    everything = pl.pallas_call(
        lambda *refs: spread_kernel(depth, *refs),
        out_shape=jax.ShapeDtypeStruct(shape, own.dtype),
        in_specs=[pl.BlockSpec(memory_space=pl.ANY)],
        out_specs=pl.BlockSpec(memory_space=pl.ANY),
        scratch_shapes=[
            pltpu.SemaphoreType.DMA,
            pltpu.SemaphoreType.DMA((depth,)),
            pltpu.SemaphoreType.DMA((depth,)),
            pltpu.SemaphoreType.DMA((7 * depth,)),
            pltpu.SemaphoreType.DMA((7 * depth,)),
        ],
        compiler_params=pltpu.CompilerParams(collective_id=0, has_side_effects=True),
        cost_estimate=pl.CostEstimate(flops=0, bytes_accessed=1 << 26, transcendentals=0),
    )(own)
    return everything.reshape((seq_count, heads) + own.shape)


def collect_kernel(
    depth,
    attn_scale,
    part_ref,
    out_grad_ref,
    query_ref,
    key_ref,
    value_ref,
    prefix_ref,
    after_ref,
    grad_query_ref,
    grad_key_ref,
    grad_value_ref,
    grad_ref,
    later_ref,
    core_got,
    one,
    one_got,
    two,
    two_got,
    three,
    three_got,
    state_out,
    state_x,
    pair_out,
    pair_got,
    send_sems,
    recv_sems,
    state_send,
    state_recv,
):
    z, x, y, c = place_of(depth)
    sibling, first, second = partners_of(z, x, y, c)
    mine_a = (1 - c) * y + c * x
    mine_b = c * y + (1 - c) * x
    greet(depth, z, x, y, c)
    copies = []
    order = list(range(depth - 1, -1, -1))

    def start(kind, k, source, target, device):
        at = kind * depth + k
        copy = send(source, target, send_sems.at[at], recv_sems.at[at], device)
        copies.append(copy)
        return copy

    core, step_a, step_b, step_z = {}, {}, {}, {}
    for k in order:
        zi = turned(depth, z, k)
        core[k] = start(0, k, part_ref.at[zi, :, :, 1 - c], core_got.at[k], sibling)
    for k in order:
        zi = turned(depth, z, k)
        core[k].wait_recv()
        for a in range(2):
            for b in range(2):
                at_x, at_y = c * a + (1 - c) * b, (1 - c) * a + c * b
                total = part_ref[zi, at_x, at_y, c].astype(jnp.float32)
                total = total + core_got[k, at_x, at_y].astype(jnp.float32)
                one[k, a, b] = total.astype(jnp.bfloat16)
        step_a[k] = start(1, k, one.at[k, 1 - mine_a], one_got.at[k], first)
    for k in order:
        step_a[k].wait_recv()
        total = one[k, mine_a].astype(jnp.float32) + one_got[k].astype(jnp.float32)
        two[k] = total.astype(jnp.bfloat16)
        step_b[k] = start(2, k, two.at[k, 1 - mine_b], two_got.at[k], second)
    for k in order:
        step_b[k].wait_recv()
        total = two[k, mine_b].astype(jnp.float32) + two_got[k].astype(jnp.float32)
        if k:
            three[k] = total.astype(jnp.bfloat16)
            device = device_of(turned(depth, z, k), x, y, c)
            step_z[k] = start(3, k, three.at[k], three_got.at[k], device)
        else:
            grad_ref[...] = out_grad_ref[...] + total
    for k in range(1, depth):
        step_z[k].wait_recv()
        grad_ref[...] += three_got[k].astype(jnp.float32)

    heads = later_ref.shape[0]
    rows = grad_ref.shape[0]
    causal = lax.broadcasted_iota(jnp.int32, (rows, rows), 0) >= lax.broadcasted_iota(
        jnp.int32, (rows, rows), 1
    )
    for h in range(heads):
        cols = pl.ds(h * HD, HD)
        later_ref[h] = fine_dot(query_ref[:, cols], grad_ref[:, cols], TN)

    def inside(h):
        cols = pl.ds(h * HD, HD)
        grad, query, key, value = (
            grad_ref[:, cols],
            query_ref[:, cols],
            key_ref[:, cols],
            value_ref[:, cols],
        )
        score_grad = jnp.where(causal, fine_dot(grad, value, NT), 0.0)
        score_match = jnp.where(causal, fine_dot(query, key, NT), 0.0)
        grad_query = fine_dot(score_grad, key, NN) + fine_dot(grad, prefix_ref[h], NT)
        grad_query_ref[:, cols] = grad_query * attn_scale
        grad_key_ref[:, cols] = fine_dot(score_grad, query, TN)
        grad_value_ref[:, cols] = fine_dot(score_match, grad, TN)

    state_out[...] = later_ref[...].astype(jnp.bfloat16)
    swap = send(
        state_out,
        state_x,
        state_send.at[0],
        state_recv.at[0],
        device_of(z, 1 - x, y, c),
    )
    copies.append(swap)
    for h in range(heads // 2):
        inside(h)
    swap.wait_recv()
    got = state_x[...].astype(jnp.float32)
    pair_out[...] = (later_ref[...] + got).astype(jnp.bfloat16)
    shared = []
    for k in range(1, depth):
        device = device_of(turned(depth, z, k), x, y, c)
        shared.append(
            send(pair_out, pair_got.at[k], state_send.at[k], state_recv.at[k], device)
        )
    for h in range(heads // 2, heads):
        inside(h)
    later_ref[...] = after_ref[...] + got * (1 - x).astype(jnp.float32)
    for k in range(1, depth):
        shared[k - 1].wait_recv()
        counted = (turned(depth, z, k, True) > z).astype(jnp.float32)
        later_ref[...] += pair_got[k].astype(jnp.float32) * counted
    for h in range(heads):
        cols = pl.ds(h * HD, HD)
        grad_key = grad_key_ref[:, cols] + fine_dot(value_ref[:, cols], later_ref[h], NT)
        grad_key_ref[:, cols] = grad_key * attn_scale
        grad_value = grad_value_ref[:, cols] + fine_dot(key_ref[:, cols], later_ref[h], NN)
        grad_value_ref[:, cols] = grad_value * attn_scale
    for copy in copies + shared:
        copy.wait_send()


def collect(part, out_grad, query_in, key_in, value_in, prefix, after, attn_scale):
    seq_count, heads, rows, feat = part.shape
    depth = seq_count // 2
    part = part.reshape(depth, 2, 2, 2, rows, feat)
    state = (feat // HD, HD, HD)
    kind = jnp.bfloat16
    return pl.pallas_call(
        lambda *refs: collect_kernel(depth, attn_scale, *refs),
        out_shape=[jax.ShapeDtypeStruct((rows, feat), jnp.float32)] * 3,
        in_specs=[pl.BlockSpec(memory_space=pltpu.VMEM)] * 7,
        out_specs=[pl.BlockSpec(memory_space=pltpu.VMEM)] * 3,
        scratch_shapes=[
            pltpu.VMEM((rows, feat), jnp.float32),
            pltpu.VMEM(state, jnp.float32),
            pltpu.VMEM((depth, 2, 2, rows, feat), kind),
            pltpu.VMEM((depth, 2, 2, rows, feat), kind),
            pltpu.VMEM((depth, 2, rows, feat), kind),
            pltpu.VMEM((depth, 2, rows, feat), kind),
            pltpu.VMEM((depth, rows, feat), kind),
            pltpu.VMEM((depth, rows, feat), kind),
            pltpu.VMEM((depth, rows, feat), kind),
            pltpu.VMEM(state, kind),
            pltpu.VMEM(state, kind),
            pltpu.VMEM(state, kind),
            pltpu.VMEM((depth,) + state, kind),
            pltpu.SemaphoreType.DMA((4 * depth,)),
            pltpu.SemaphoreType.DMA((4 * depth,)),
            pltpu.SemaphoreType.DMA((depth,)),
            pltpu.SemaphoreType.DMA((depth,)),
        ],
        compiler_params=pltpu.CompilerParams(
            collective_id=1, has_side_effects=True, vmem_limit_bytes=56 * 1024 * 1024
        ),
        cost_estimate=pl.CostEstimate(flops=0, bytes_accessed=1 << 26, transcendentals=0),
    )(part, out_grad, query_in, key_in, value_in, prefix, after)


def route_table(expert_ids, route_weights):
    tok_rows = expert_ids.shape[0]
    named = (expert_ids.T[:, None, :] == jnp.arange(EXPERTS, dtype=jnp.int32)[None, :, None])
    mask = jnp.any(named, axis=0)
    weight = jnp.sum(jnp.where(named, route_weights.T[:, None, :], 0.0), axis=0)
    before = jnp.arange(tok_rows)[:, None] < jnp.arange(tok_rows)[None, :]
    rank = jnp.dot(
        mask.astype(jnp.bfloat16), before.astype(jnp.bfloat16), preferred_element_type=jnp.float32
    )
    rank = jnp.where(mask, rank, -1.0)
    return jnp.concatenate([rank, weight], axis=0).astype(jnp.bfloat16)


def per_device(
    hidden_in,
    out_grad,
    expert_ids,
    route_weights,
    w_gate,
    w_up,
    w_down,
    query_in,
    key_in,
    value_in,
    state_before,
    grad_after,
):
    seq_count = lax.axis_size("seq")
    heads = lax.axis_size("head")
    tok_rows = expert_ids.shape[0]
    head_local = query_in.shape[1] // HD
    sent = jnp.concatenate(
        [
            hidden_in,
            out_grad.astype(jnp.bfloat16),
            route_table(expert_ids, route_weights),
        ],
        axis=1,
    )
    if heads == 4 and seq_count % 2 == 0:
        x_all = spread(sent, seq_count, heads)
    else:
        x_all = lax.all_gather(sent, ("seq", "head"))
        x_all = x_all.reshape(seq_count, heads, tok_rows, sent.shape[1])
    query_heads = query_in.reshape(tok_rows, head_local, HD)
    key_heads = key_in.reshape(tok_rows, head_local, HD)
    value_heads = value_in.reshape(tok_rows, head_local, HD)
    kv_local = jnp.einsum("shi,shj->hij", key_heads, value_heads, precision=HIGHEST)
    prefix = carried_in(kv_local, "seq", False) + state_before
    grad_gate, grad_up, grad_down, part = expert_call(x_all, w_gate, w_up, w_down)
    attn_scale = (HD * tok_rows * seq_count) ** (-0.5)
    if heads == 4 and seq_count % 2 == 0:
        grad_query, grad_key, grad_value = collect(
            part, out_grad, query_in, key_in, value_in, prefix, grad_after, attn_scale
        )
    else:
        part = part.reshape(seq_count * heads, tok_rows, -1)
        moe_grad = lax.psum_scatter(part, ("seq", "head"), scatter_dimension=0, tiled=True)
        moe_grad = moe_grad.reshape(tok_rows, -1).astype(jnp.float32)
        attn_grad = (out_grad + moe_grad).reshape(tok_rows, head_local, HD)
        qd_local = jnp.einsum("thi,thj->hij", query_heads, attn_grad, precision=HIGHEST)
        suffix = carried_in(qd_local, "seq", True) + grad_after
        grad_query, grad_key, grad_value = attention_backward(
            query_heads, key_heads, value_heads, attn_grad, prefix, suffix, attn_scale
        )
    return (
        grad_gate,
        grad_up,
        grad_down,
        grad_query.reshape(tok_rows, -1),
        grad_key.reshape(tok_rows, -1),
        grad_value.reshape(tok_rows, -1),
    )


def solution(mesh):
    placed = (
        P("seq", "head"),
        P("seq", "head"),
        P("seq", None),
        P("seq", None),
        P("seq", None, "head"),
        P("seq", None, "head"),
        P("seq", "head", None),
        P("seq", "head"),
        P("seq", "head"),
        P("seq", "head"),
        P("head", None, None),
        P("head", None, None),
    )
    return jax.shard_map(
        per_device,
        mesh=mesh,
        in_specs=placed,
        out_specs=(
            P("seq", None, "head"),
            P("seq", None, "head"),
            P("seq", "head", None),
            P("seq", "head"),
            P("seq", "head"),
            P("seq", "head"),
        ),
        check_vma=False,
    )
```

```python
import jax
import jax.numpy as jnp
from jax import lax
from jax.experimental import pallas as pl
from jax.experimental.pallas import tpu as pltpu
from jax.sharding import PartitionSpec as P

EXPERTS = 64
TOPK = 8
HD = 128
CAP = 32


HIGHEST = lax.Precision.HIGHEST
MESH = pl.DeviceIdType.MESH


def carried_in(shard, axis, backward):
    place = lax.axis_index(axis)
    gathered = lax.all_gather(shard.astype(jnp.bfloat16), axis).astype(jnp.float32)
    order = jnp.arange(gathered.shape[0])
    used = (order > place) if backward else (order < place)
    return jnp.sum(jnp.where(used[:, None, None, None], gathered, 0.0), axis=0)


def attention_backward(query_in, key_in, value_in, attn_grad, prefix, suffix, attn_scale):
    block_len = query_in.shape[0]
    causal = jnp.arange(block_len)[:, None] >= jnp.arange(block_len)[None, :]
    score_grad = jnp.einsum("thj,shj->hts", attn_grad, value_in, precision=HIGHEST)
    score_grad = jnp.where(causal[None], score_grad, 0.0)
    score_match = jnp.einsum("thi,shi->hts", query_in, key_in, precision=HIGHEST)
    score_match = jnp.where(causal[None], score_match, 0.0)
    grad_query = jnp.einsum("hts,shi->thi", score_grad, key_in, precision=HIGHEST)
    grad_query = grad_query + jnp.einsum("thj,hij->thi", attn_grad, prefix, precision=HIGHEST)
    grad_key = jnp.einsum("hts,thi->shi", score_grad, query_in, precision=HIGHEST)
    grad_key = grad_key + jnp.einsum("shj,hij->shi", value_in, suffix, precision=HIGHEST)
    grad_value = jnp.einsum("hts,thj->shj", score_match, attn_grad, precision=HIGHEST)
    grad_value = grad_value + jnp.einsum("shi,hij->shj", key_in, suffix, precision=HIGHEST)
    return (grad_query * attn_scale, grad_key * attn_scale, grad_value * attn_scale)


NN = (((1,), (0,)), ((), ()))
NT = (((1,), (1,)), ((), ()))
TN = (((0,), (0,)), ((), ()))


def dot(a, b, dims=NN):
    return lax.dot_general(a, b, dims, preferred_element_type=jnp.float32)


def expert_kernel(
    seq_count,
    exp_local,
    x_ref,
    wg_ref,
    wu_ref,
    wd_ref,
    gg_ref,
    gu_ref,
    gd_ref,
    part_ref,
    rows,
    grads,
    picks,
    route,
):
    step = pl.program_id(0)
    heads = x_ref.shape[0]
    tok_rows, feat = part_ref.shape[2:]
    lanes = x_ref.shape[2]
    chunks = feat // lanes
    share = 2 * EXPERTS // heads

    def features(h, first):
        parts = [
            x_ref[h, (first + j) * tok_rows : (first + j + 1) * tok_rows, :]
            for j in range(chunks)
        ]
        return jnp.concatenate(parts, axis=1)

    @pl.when(step < seq_count)
    def _gather():
        base = lax.axis_index("seq") * exp_local
        for h in range(heads):
            table = x_ref[h, 2 * chunks * tok_rows :, :].astype(jnp.float32)
            route[h * share : (h + 1) * share, :] = table
        ranks = lax.broadcasted_iota(jnp.int32, (CAP, tok_rows), 0).astype(jnp.float32)
        ones, scaled = [], []
        for e in range(exp_local):
            rank_row = route[pl.ds(base + e, 1), :]
            weight_row = route[pl.ds(EXPERTS + base + e, 1), :]
            hit = ranks == rank_row
            ones.append(jnp.where(hit, 1.0, 0.0))
            scaled.append(jnp.where(hit, weight_row, 0.0))
        one = jnp.concatenate(ones, axis=0).astype(jnp.bfloat16)
        weighted = jnp.concatenate(scaled, axis=0).astype(jnp.bfloat16)
        picks[step] = one
        at = pl.ds(pl.multiple_of(step * CAP, CAP), CAP)
        for h in range(heads):
            cols = pl.ds(h * feat, feat)
            got = dot(one, features(h, 0)).astype(jnp.bfloat16)
            rows[:, at, cols] = got.reshape(exp_local, CAP, feat)
            got = dot(weighted, features(h, chunks)).astype(jnp.bfloat16)
            grads[:, at, cols] = got.reshape(exp_local, CAP, feat)

    @pl.when((step >= seq_count) & (step < seq_count + exp_local))
    def _expert():
        e = step - seq_count
        xr = rows[e]
        gr = grads[e]
        wg = wg_ref[0]
        wu = wu_ref[0]
        pre_gate = dot(xr, wg)
        pre_up = dot(xr, wu)
        d_inner = dot(gr, wd_ref[0], NT)
        sig = jax.nn.sigmoid(pre_gate)
        swish = pre_gate * sig
        act = (swish * pre_up).astype(jnp.bfloat16)
        d_gate = (d_inner * pre_up * sig * (1.0 + pre_gate * (1.0 - sig))).astype(jnp.bfloat16)
        d_up = (d_inner * swish).astype(jnp.bfloat16)
        gd_ref[0] = dot(act, gr, TN).astype(jnp.bfloat16)
        gg_ref[0] = dot(xr, d_gate, TN).astype(jnp.bfloat16)
        gu_ref[0] = dot(xr, d_up, TN).astype(jnp.bfloat16)
        rows[e] = (dot(d_gate, wg, NT) + dot(d_up, wu, NT)).astype(jnp.bfloat16)

    @pl.when(step >= seq_count + exp_local)
    def _combine():
        b = step - seq_count - exp_local
        at = pl.ds(pl.multiple_of(b * CAP, CAP), CAP)
        for h in range(heads):
            back = rows[:, at, pl.ds(h * feat, feat)].reshape(exp_local * CAP, feat)
            part_ref[0, h] = dot(picks[b], back, TN).astype(jnp.bfloat16)


def expert_call(x_all, w_gate, w_up, w_down):
    seq_count, heads, packed, tok_rows = x_all.shape
    exp_local, model, hidden = w_gate.shape
    feat = model // heads
    slots = seq_count * CAP

    def expert_at(i):
        return (jnp.clip(i - seq_count, 0, exp_local - 1), 0, 0)

    def block_in(i):
        return (jnp.minimum(i, seq_count - 1), 0, 0, 0)

    def block_out(i):
        return (jnp.maximum(i - seq_count - exp_local, 0), 0, 0, 0)

    tall = pl.BlockSpec((1, model, hidden), expert_at)
    flat = pl.BlockSpec((1, hidden, model), expert_at)
    return pl.pallas_call(
        lambda *refs: expert_kernel(seq_count, exp_local, *refs),
        grid=(2 * seq_count + exp_local,),
        in_specs=[pl.BlockSpec((None, heads, packed, tok_rows), block_in), tall, tall, flat],
        out_specs=[tall, tall, flat, pl.BlockSpec((1, heads, tok_rows, feat), block_out)],
        out_shape=[
            jax.ShapeDtypeStruct(w_gate.shape, jnp.bfloat16),
            jax.ShapeDtypeStruct(w_up.shape, jnp.bfloat16),
            jax.ShapeDtypeStruct(w_down.shape, jnp.bfloat16),
            jax.ShapeDtypeStruct((seq_count, heads, tok_rows, feat), jnp.bfloat16),
        ],
        scratch_shapes=[
            pltpu.VMEM((exp_local, slots, model), jnp.bfloat16),
            pltpu.VMEM((exp_local, slots, model), jnp.bfloat16),
            pltpu.VMEM((seq_count, exp_local * CAP, tok_rows), jnp.bfloat16),
            pltpu.VMEM((2 * EXPERTS, tok_rows), jnp.float32),
        ],
        compiler_params=pltpu.CompilerParams(vmem_limit_bytes=56 * 1024 * 1024),
        cost_estimate=pl.CostEstimate(
            flops=16 * exp_local * slots * model * hidden,
            bytes_accessed=12 * exp_local * model * hidden,
            transcendentals=0,
        ),
    )(x_all, w_gate, w_up, w_down)


def fine_dot(a, b, dims):
    return lax.dot_general(a, b, dims, precision=HIGHEST, preferred_element_type=jnp.float32)


def place_of(depth):
    s, h = lax.axis_index("seq"), lax.axis_index("head")
    return s // 2, s % 2, h // 2, h % 2


def device_of(z, x, y, c):
    return (z * 2 + x, y * 2 + c)


def turned(depth, z, k, back=False):
    if depth & (depth - 1):
        return (z + (depth - k if back else k)) % depth
    result, bit = 0, 1
    while bit < depth:
        own = (z // bit) % 2
        result = result + bit * (1 - own if k & bit else own)
        bit *= 2
    return result


def partners_of(z, x, y, c):
    other_x, other_y = 1 - x, 1 - y
    sibling = device_of(z, x, y, 1 - c)
    first = device_of(z, c * other_x + (1 - c) * x, (1 - c) * other_y + c * y, c)
    second = device_of(z, (1 - c) * other_x + c * x, c * other_y + (1 - c) * y, c)
    return sibling, first, second


def greet(depth, z, x, y, c):
    barrier = pltpu.get_barrier_semaphore()
    known = list(partners_of(z, x, y, c))
    known += [device_of(turned(depth, z, k), x, y, c) for k in range(1, depth)]
    for device in known:
        pl.semaphore_signal(barrier, inc=1, device_id=device, device_id_type=MESH)
    pl.semaphore_wait(barrier, len(known))


def send(source, target, send_sem, recv_sem, device):
    copy = pltpu.make_async_remote_copy(
        src_ref=source,
        dst_ref=target,
        send_sem=send_sem,
        recv_sem=recv_sem,
        device_id=device,
        device_id_type=MESH,
    )
    copy.start()
    return copy


def spread_kernel(depth, own_ref, all_ref, local_sem, z_send, z_recv, p_send, p_recv):
    z, x, y, c = place_of(depth)
    sibling, first, second = partners_of(z, x, y, c)
    mine_a = (1 - c) * y + c * x
    mine_b = c * y + (1 - c) * x

    def slot(zi, a, b):
        return all_ref.at[zi, c * a + (1 - c) * b, (1 - c) * a + c * b, c]

    greet(depth, z, x, y, c)
    local = pltpu.make_async_copy(own_ref, slot(z, mine_a, mine_b), local_sem)
    local.start()
    along = [None] * depth
    for k in range(1, depth):
        along[k] = send(
            own_ref,
            slot(z, mine_a, mine_b),
            z_send.at[k],
            z_recv.at[k],
            device_of(turned(depth, z, k), x, y, c),
        )
    sent = {}

    def start(kind, k, source, target, device):
        at = kind * depth + k
        sent[kind, k] = send(source, target, p_send.at[at], p_recv.at[at], device)

    def arrive_z(k):
        target = slot(turned(depth, z, k, True), mine_a, mine_b)
        if k:
            along[k].wait_recv()
        source = target if k else own_ref
        start(0, k, source, target, first)
        start(1, k, source, target, second)
        start(3, k, source, target, sibling)

    def arrive_first(k):
        sent[0, k].wait_recv()
        target = slot(turned(depth, z, k, True), 1 - mine_a, mine_b)
        start(2, k, target, target, second)
        start(4, k, target, target, sibling)

    for t in range(depth + 1):
        if t < depth:
            arrive_z(t)
        if t:
            arrive_first(t - 1)
    for kind, a in ((1, mine_a), (2, 1 - mine_a)):
        for k in range(depth):
            sent[kind, k].wait_recv()
            target = slot(turned(depth, z, k, True), a, 1 - mine_b)
            start(kind + 4, k, target, target, sibling)
    for kind in (3, 4, 5, 6):
        for k in range(depth):
            sent[kind, k].wait_recv()
    for k in range(1, depth):
        along[k].wait_send()
    for copy in sent.values():
        copy.wait_send()
    local.wait()


def spread(own, seq_count, heads):
    depth = seq_count // 2
    shape = (depth, 2, 2, 2) + own.shape
    everything = pl.pallas_call(
        lambda *refs: spread_kernel(depth, *refs),
        out_shape=jax.ShapeDtypeStruct(shape, own.dtype),
        in_specs=[pl.BlockSpec(memory_space=pl.ANY)],
        out_specs=pl.BlockSpec(memory_space=pl.ANY),
        scratch_shapes=[
            pltpu.SemaphoreType.DMA,
            pltpu.SemaphoreType.DMA((depth,)),
            pltpu.SemaphoreType.DMA((depth,)),
            pltpu.SemaphoreType.DMA((7 * depth,)),
            pltpu.SemaphoreType.DMA((7 * depth,)),
        ],
        compiler_params=pltpu.CompilerParams(collective_id=0, has_side_effects=True),
        cost_estimate=pl.CostEstimate(flops=0, bytes_accessed=1 << 26, transcendentals=0),
    )(own)
    return everything.reshape((seq_count, heads) + own.shape)


def collect_kernel(
    depth,
    part_ref,
    out_grad_ref,
    query_ref,
    key_ref,
    value_ref,
    prefix_ref,
    after_ref,
    grad_query_ref,
    grad_key_ref,
    grad_value_ref,
    grad_ref,
    later_ref,
    core_got,
    one,
    one_got,
    two,
    two_got,
    three,
    three_got,
    state_out,
    state_x,
    pair_out,
    pair_got,
    send_sems,
    recv_sems,
    state_send,
    state_recv,
):
    z, x, y, c = place_of(depth)
    sibling, first, second = partners_of(z, x, y, c)
    mine_a = (1 - c) * y + c * x
    mine_b = c * y + (1 - c) * x
    greet(depth, z, x, y, c)
    copies = []
    order = list(range(depth - 1, -1, -1))

    def start(kind, k, source, target, device):
        at = kind * depth + k
        copy = send(source, target, send_sems.at[at], recv_sems.at[at], device)
        copies.append(copy)
        return copy

    core, step_a, step_b, step_z = {}, {}, {}, {}
    for k in order:
        zi = turned(depth, z, k)
        core[k] = start(0, k, part_ref.at[zi, :, :, 1 - c], core_got.at[k], sibling)
    for k in order:
        zi = turned(depth, z, k)
        core[k].wait_recv()
        for a in range(2):
            for b in range(2):
                at_x, at_y = c * a + (1 - c) * b, (1 - c) * a + c * b
                total = part_ref[zi, at_x, at_y, c].astype(jnp.float32)
                total = total + core_got[k, at_x, at_y].astype(jnp.float32)
                one[k, a, b] = total.astype(jnp.bfloat16)
        step_a[k] = start(1, k, one.at[k, 1 - mine_a], one_got.at[k], first)
    for k in order:
        step_a[k].wait_recv()
        total = one[k, mine_a].astype(jnp.float32) + one_got[k].astype(jnp.float32)
        two[k] = total.astype(jnp.bfloat16)
        step_b[k] = start(2, k, two.at[k, 1 - mine_b], two_got.at[k], second)
    for k in order:
        step_b[k].wait_recv()
        total = two[k, mine_b].astype(jnp.float32) + two_got[k].astype(jnp.float32)
        if k:
            three[k] = total.astype(jnp.bfloat16)
            device = device_of(turned(depth, z, k), x, y, c)
            step_z[k] = start(3, k, three.at[k], three_got.at[k], device)
        else:
            grad_ref[...] = out_grad_ref[...] + total
    for k in range(1, depth):
        step_z[k].wait_recv()
        grad_ref[...] += three_got[k].astype(jnp.float32)

    heads = later_ref.shape[0]
    rows = grad_ref.shape[0]
    causal = lax.broadcasted_iota(jnp.int32, (rows, rows), 0) >= lax.broadcasted_iota(
        jnp.int32, (rows, rows), 1
    )
    for h in range(heads):
        cols = pl.ds(h * HD, HD)
        later_ref[h] = fine_dot(query_ref[:, cols], grad_ref[:, cols], TN)

    def inside(h):
        cols = pl.ds(h * HD, HD)
        grad, query, key, value = (
            grad_ref[:, cols],
            query_ref[:, cols],
            key_ref[:, cols],
            value_ref[:, cols],
        )
        score_grad = jnp.where(causal, fine_dot(grad, value, NT), 0.0)
        score_match = jnp.where(causal, fine_dot(query, key, NT), 0.0)
        grad_query = fine_dot(score_grad, key, NN) + fine_dot(grad, prefix_ref[h], NT)
        grad_query_ref[:, cols] = grad_query
        grad_key_ref[:, cols] = fine_dot(score_grad, query, TN)
        grad_value_ref[:, cols] = fine_dot(score_match, grad, TN)

    state_out[...] = later_ref[...].astype(jnp.bfloat16)
    swap = send(
        state_out,
        state_x,
        state_send.at[0],
        state_recv.at[0],
        device_of(z, 1 - x, y, c),
    )
    copies.append(swap)
    for h in range(heads // 2):
        inside(h)
    swap.wait_recv()
    got = state_x[...].astype(jnp.float32)
    pair_out[...] = (later_ref[...] + got).astype(jnp.bfloat16)
    shared = []
    for k in range(1, depth):
        device = device_of(turned(depth, z, k), x, y, c)
        shared.append(
            send(pair_out, pair_got.at[k], state_send.at[k], state_recv.at[k], device)
        )
    for h in range(heads // 2, heads):
        inside(h)
    later_ref[...] = after_ref[...] + got * (1 - x).astype(jnp.float32)
    for k in range(1, depth):
        shared[k - 1].wait_recv()
        counted = (turned(depth, z, k, True) > z).astype(jnp.float32)
        later_ref[...] += pair_got[k].astype(jnp.float32) * counted
    for h in range(heads):
        cols = pl.ds(h * HD, HD)
        grad_key = grad_key_ref[:, cols] + fine_dot(value_ref[:, cols], later_ref[h], NT)
        grad_key_ref[:, cols] = grad_key
        grad_value = grad_value_ref[:, cols] + fine_dot(key_ref[:, cols], later_ref[h], NN)
        grad_value_ref[:, cols] = grad_value
    for copy in copies + shared:
        copy.wait_send()


def collect(part, out_grad, query_in, key_in, value_in, prefix, after):
    seq_count, heads, rows, feat = part.shape
    depth = seq_count // 2
    part = part.reshape(depth, 2, 2, 2, rows, feat)
    state = (feat // HD, HD, HD)
    kind = jnp.bfloat16
    return pl.pallas_call(
        lambda *refs: collect_kernel(depth, *refs),
        out_shape=[jax.ShapeDtypeStruct((rows, feat), jnp.float32)] * 3,
        in_specs=[pl.BlockSpec(memory_space=pltpu.VMEM)] * 7,
        out_specs=[pl.BlockSpec(memory_space=pltpu.VMEM)] * 3,
        scratch_shapes=[
            pltpu.VMEM((rows, feat), jnp.float32),
            pltpu.VMEM(state, jnp.float32),
            pltpu.VMEM((depth, 2, 2, rows, feat), kind),
            pltpu.VMEM((depth, 2, 2, rows, feat), kind),
            pltpu.VMEM((depth, 2, rows, feat), kind),
            pltpu.VMEM((depth, 2, rows, feat), kind),
            pltpu.VMEM((depth, rows, feat), kind),
            pltpu.VMEM((depth, rows, feat), kind),
            pltpu.VMEM((depth, rows, feat), kind),
            pltpu.VMEM(state, kind),
            pltpu.VMEM(state, kind),
            pltpu.VMEM(state, kind),
            pltpu.VMEM((depth,) + state, kind),
            pltpu.SemaphoreType.DMA((4 * depth,)),
            pltpu.SemaphoreType.DMA((4 * depth,)),
            pltpu.SemaphoreType.DMA((depth,)),
            pltpu.SemaphoreType.DMA((depth,)),
        ],
        compiler_params=pltpu.CompilerParams(
            collective_id=1, has_side_effects=True, vmem_limit_bytes=56 * 1024 * 1024
        ),
        cost_estimate=pl.CostEstimate(flops=0, bytes_accessed=1 << 26, transcendentals=0),
    )(part, out_grad, query_in, key_in, value_in, prefix, after)


def route_table(expert_ids, route_weights):
    tok_rows = expert_ids.shape[0]
    named = (expert_ids.T[:, None, :] == jnp.arange(EXPERTS, dtype=jnp.int32)[None, :, None])
    mask = jnp.any(named, axis=0)
    weight = jnp.sum(jnp.where(named, route_weights.T[:, None, :], 0.0), axis=0)
    before = jnp.arange(tok_rows)[:, None] < jnp.arange(tok_rows)[None, :]
    rank = jnp.dot(
        mask.astype(jnp.bfloat16), before.astype(jnp.bfloat16), preferred_element_type=jnp.float32
    )
    rank = jnp.where(mask, rank, -1.0)
    return jnp.concatenate([rank, weight], axis=0).astype(jnp.bfloat16)


def in_chunks(array):
    rows, width = array.shape
    return array.reshape(rows, width // rows, rows).transpose(1, 0, 2).reshape(-1, rows)


def per_device(
    hidden_in,
    out_grad,
    expert_ids,
    route_weights,
    w_gate,
    w_up,
    w_down,
    query_in,
    key_in,
    value_in,
    state_before,
    grad_after,
):
    seq_count = lax.axis_size("seq")
    heads = lax.axis_size("head")
    tok_rows = expert_ids.shape[0]
    head_local = query_in.shape[1] // HD
    table = route_table(expert_ids, route_weights)
    share = table.shape[0] // heads
    sent = jnp.concatenate(
        [
            in_chunks(hidden_in),
            in_chunks(out_grad.astype(jnp.bfloat16)),
            lax.dynamic_slice_in_dim(table, lax.axis_index("head") * share, share, 0),
        ],
        axis=0,
    )
    if heads == 4 and seq_count % 2 == 0:
        x_all = spread(sent, seq_count, heads)
    else:
        x_all = lax.all_gather(sent, ("seq", "head"))
        x_all = x_all.reshape((seq_count, heads) + sent.shape)
    query_heads = query_in.reshape(tok_rows, head_local, HD)
    key_heads = key_in.reshape(tok_rows, head_local, HD)
    value_heads = value_in.reshape(tok_rows, head_local, HD)
    kv_local = jnp.einsum("shi,shj->hij", key_heads, value_heads, precision=HIGHEST)
    prefix = carried_in(kv_local, "seq", False) + state_before
    grad_gate, grad_up, grad_down, part = expert_call(x_all, w_gate, w_up, w_down)
    attn_scale = (HD * tok_rows * seq_count) ** (-0.5)
    if heads == 4 and seq_count % 2 == 0:
        grad_query, grad_key, grad_value = collect(
            part, out_grad, query_in, key_in, value_in, prefix, grad_after
        )
        grad_query, grad_key, grad_value = (
            grad_query * attn_scale,
            grad_key * attn_scale,
            grad_value * attn_scale,
        )
    else:
        part = part.reshape(seq_count * heads, tok_rows, -1)
        moe_grad = lax.psum_scatter(part, ("seq", "head"), scatter_dimension=0, tiled=True)
        moe_grad = moe_grad.reshape(tok_rows, -1).astype(jnp.float32)
        attn_grad = (out_grad + moe_grad).reshape(tok_rows, head_local, HD)
        qd_local = jnp.einsum("thi,thj->hij", query_heads, attn_grad, precision=HIGHEST)
        suffix = carried_in(qd_local, "seq", True) + grad_after
        grad_query, grad_key, grad_value = attention_backward(
            query_heads, key_heads, value_heads, attn_grad, prefix, suffix, attn_scale
        )
    return (
        grad_gate,
        grad_up,
        grad_down,
        grad_query.reshape(tok_rows, -1),
        grad_key.reshape(tok_rows, -1),
        grad_value.reshape(tok_rows, -1),
    )


def solution(mesh):
    placed = (
        P("seq", "head"),
        P("seq", "head"),
        P("seq", None),
        P("seq", None),
        P("seq", None, "head"),
        P("seq", None, "head"),
        P("seq", "head", None),
        P("seq", "head"),
        P("seq", "head"),
        P("seq", "head"),
        P("head", None, None),
        P("head", None, None),
    )
    return jax.shard_map(
        per_device,
        mesh=mesh,
        in_specs=placed,
        out_specs=(
            P("seq", None, "head"),
            P("seq", None, "head"),
            P("seq", "head", None),
            P("seq", "head"),
            P("seq", "head"),
            P("seq", "head"),
        ),
        check_vma=False,
    )
```
